32 devices in a mesh: seq: 2 (over x), row: 16 (over z, y, core).
Axes of the slice: x: 2, y: 2, z: 4, core: 2. Of those that a mesh axis runs over, the one named last changes fastest.
Arguments:
- qm: float32 [2, 16, 7, 256, 256], P('seq', 'row'), parts along dimension 0, may hold values from 0.005 to 0.05
- qm1: float32 [2, 16, 7, 256, 256], P('seq', 'row'), parts along dimension 0, may hold values from 0.005 to 0.05
- qb: float32 [2, 16, 7, 256, 256], P('seq', 'row'), parts along dimension 0, may hold values from 0.05 to 2
- codes: int32 [2, 16, 256], P('seq', 'row'), parts along dimension 0, may hold values from 0 to 3
- energy_index: int32 [2, 16, 256, 256], P('seq', 'row'), parts along dimension 0, may hold values from 0 to 63
- turner: float32 [64], replicated, may hold values from -1 to 1.5
Outputs:
- qb_new: float32 [2, 16, 256, 256], P('seq', 'row'), parts along dimension 0
- qm1_new: float32 [2, 16, 256, 256], P('seq', 'row'), parts along dimension 0
- qm_new: float32 [2, 16, 256, 256], P('seq', 'row'), parts along dimension 0
The draws below stay inside these ranges and needn't reach their ends.
There are 2 independent parts, one for each index of `seq`. The reference program is written for one: setup_inputs(seed, part) draws one part's arguments, and reference() takes and returns one part's arrays. A program takes and returns all parts, laid end to end along the dimension named above; an argument that names none is the same for every part. Nothing has to cross between parts.
All inputs are finite; a program needn't handle non-finite values.
Results may differ from the reference program's by a relative error of at most 0.0003.
Values sent between devices are 32-bit elements; how exact they have to be, the bound alone decides.
No kernel may reach another device: no remote copies, remote signals or barrier semaphores. Data moves between devices by JAX's collectives and lax.ppermute only.
A program may use at most 64 MiB of HBM per device.

```python
import math
import jax
import jax.numpy as jnp
import numpy as np
from jax import lax

B = 256
DIST = 8
CYCLES = 1
TABLE = 64
DM = 7
BLOCK_ROWS = 16


def plant(entries, own_key, smallest, top_value):
    index_at = [jax.random.randint(jax.random.fold_in(own_key, axis), (), 0, length) for axis, length in enumerate(entries.shape)]
    main_axis = entries.shape.index(max(entries.shape))
    beside = index_at[:main_axis] + [(index_at[main_axis] + 1) % entries.shape[main_axis]] + index_at[main_axis + 1:]
    return entries.at[tuple(index_at)].set(smallest).at[tuple(beside)].set(top_value)


def levels(key, extent, cuts, smallest, largest):
    factor_of, own = 1.0, jax.random.fold_in(key, 6)
    for axis_at, blocks in cuts:
        steps = jnp.exp(jax.random.uniform(jax.random.fold_in(own, axis_at), (blocks,), jnp.float32, smallest / len(cuts), largest / len(cuts)))
        factor_of = factor_of * jnp.repeat(steps, extent[axis_at] // blocks).reshape([-1 if axis == axis_at else 1 for axis in range(len(extent))])
    return factor_of


def setup_inputs(seed: int = 0, part: int = 0) -> dict:
    key_of = jax.random.split(jax.random.key(seed), 7)
    part_splits = jax.random.split(jax.random.fold_in(key_of[6], part), 7)
    qm = jnp.clip(jnp.exp(math.log(0.05) - 2.3025851 * jax.random.uniform(part_splits[0], (CYCLES, BLOCK_ROWS, DM, B, B), jnp.float32) ** levels(part_splits[0], (CYCLES, BLOCK_ROWS, DM, B, B), ((1, 16),), -0.2, 0.2)), 0.005, 0.05)
    qm1 = jnp.clip(jnp.exp(math.log(0.05) - 2.3025851 * jax.random.uniform(part_splits[1], (CYCLES, BLOCK_ROWS, DM, B, B), jnp.float32) ** levels(part_splits[1], (CYCLES, BLOCK_ROWS, DM, B, B), ((1, 16),), -0.2, 0.2)), 0.005, 0.05)
    qb = jnp.clip(jnp.exp(math.log(2.0) - 3.6888794 * jax.random.uniform(part_splits[2], (CYCLES, BLOCK_ROWS, DM, B, B), jnp.float32) ** levels(part_splits[2], (CYCLES, BLOCK_ROWS, DM, B, B), ((1, 16),), -0.2, 0.2)), 0.05, 2.0)
    codes = plant(jax.random.randint(part_splits[3], (CYCLES, BLOCK_ROWS, B), 0, 4), jax.random.fold_in(part_splits[3], 1), 0, 3).astype(jnp.int32)
    energy_index = plant(jax.random.randint(part_splits[4], (CYCLES, BLOCK_ROWS, B, B), 0, TABLE), jax.random.fold_in(part_splits[4], 1), 0, TABLE - 1).astype(jnp.int32)
    turner = jnp.clip(jax.random.uniform(key_of[5], (TABLE,), jnp.float32, -1.0, 1.5), -1.0, 1.5)
    return {"qm": qm, "qm1": qm1, "qb": qb, "codes": codes, "energy_index": energy_index, "turner": turner}


PAIRS = np.array([[0, 0, 0, 1], [0, 0, 1, 0], [0, 1, 0, 1], [1, 0, 1, 0]], dtype=np.float32)
HI = lax.Precision.HIGHEST


def unpaired(shift):
    offsets = jnp.arange(B, dtype=jnp.int32)
    diffs = (shift * B + offsets[None, :] - offsets[:, None]).astype(jnp.float32)
    values = 0.01 * jnp.exp(-diffs / (DIST * B))
    if shift == 0:
        values = jnp.where(diffs >= 0, values, jnp.float32(0.0))
    return values


def decay(level):
    offsets = jnp.arange(B, dtype=jnp.int32)
    diffs = ((DIST - level) * B + offsets[None, :] - offsets[:, None]).astype(jnp.float32)
    values = jnp.exp(-diffs / (DIST * B))
    if level == DIST:
        values = jnp.where(diffs >= 0, values, jnp.float32(0.0))
    return values


def pairing(first, second):
    table = jnp.asarray(PAIRS, dtype=jnp.float32)
    digits = jnp.arange(4, dtype=jnp.int32)
    left = (first[:, None] == digits[None, :]).astype(jnp.float32)
    right = (second[:, None] == digits[None, :]).astype(jnp.float32)
    return jnp.dot(jnp.dot(left, table, precision=HI), right.T, precision=HI)


def reference(qm, qm1, qb, codes, energy_index, turner):
    total = CYCLES * BLOCK_ROWS
    qm_flat = qm.reshape(total, DIST - 1, B, B)
    qm1_flat = qm1.reshape(total, DIST - 1, B, B)
    qb_flat = qb.reshape(total, DIST - 1, B, B)
    code_flat = codes.reshape(total, B)
    index_flat = energy_index.reshape(total, B, B)

    def one(block):
        live = block + DIST < total
        summed = jnp.zeros((B, B), jnp.float32)
        tails = jnp.zeros((B, B), jnp.float32)
        for shift in range(1, DIST):
            later = jnp.minimum(block + shift, total - 1)
            right = qm1_flat[later, DIST - shift - 1]
            summed = summed + jnp.dot(qm_flat[block, shift - 1], right, precision=HI)
            tails = tails + jnp.dot(unpaired(shift), right, precision=HI)
        closing = jnp.minimum(block + DIST, total - 1)
        allowed = pairing(code_flat[block], code_flat[closing])
        weight = jnp.exp(-jnp.take(turner, index_flat[block]))
        pair_new = allowed * weight * (1.0 + 0.8 * summed)
        branch = jnp.dot(pair_new, decay(DIST), precision=HI)
        for level in range(1, DIST):
            branch = branch + jnp.dot(qb_flat[block, level - 1], decay(level), precision=HI)
        branch = branch * (1.0 / (DIST * B))
        multi = summed + tails + jnp.dot(unpaired(0), branch, precision=HI)
        zero = jnp.float32(0.0)
        return jnp.where(live, pair_new, zero), jnp.where(live, branch, zero), jnp.where(live, multi, zero)

    pair_all, branch_all, multi_all = lax.map(one, jnp.arange(total, dtype=jnp.int32))
    shape = (CYCLES, BLOCK_ROWS, B, B)
    return pair_all.reshape(shape), branch_all.reshape(shape), multi_all.reshape(shape)
```

```python
import functools

import jax
import jax.numpy as jnp
from jax import lax
from jax.experimental import pallas as pl
from jax.experimental.pallas import tpu as pltpu
from jax.sharding import PartitionSpec as P

F32 = jnp.float32
BF16 = jnp.bfloat16
LANES = 128


def halves(x):
    high = x.astype(BF16)
    return high, (x - high.astype(F32)).astype(BF16)


def dot(a, b):
    return jnp.dot(a, b, preferred_element_type=F32)


def product(left, right):
    left_high, left_low = halves(left)
    right_high, right_low = halves(right)
    return dot(left_high, right_high) + dot(left_high, right_low) + dot(left_low, right_high)


def column(size, start, beta):
    steps = lax.broadcasted_iota(jnp.int32, (size, 1), 0) + start
    return jnp.exp(steps.astype(F32) * -beta)


def row(size, start, beta):
    steps = lax.broadcasted_iota(jnp.int32, (1, size), 1) + start
    return jnp.exp(steps.astype(F32) * -beta)


def weights_kernel(dist, index_ref, turner_ref, qb_ref, weight_ref, branch_ref):
    size = index_ref.shape[0]
    beta = 1.0 / (dist * size)
    entries = turner_ref.shape[1]
    for start in range(0, size, LANES):
        index = index_ref[:, start:start + LANES]
        found = jnp.zeros(index.shape, F32)
        for first in range(0, entries, LANES):
            table = jnp.exp(-turner_ref[:, first:first + LANES])
            table = jnp.broadcast_to(table, index.shape)
            inside = (index >= first) & (index < first + LANES)
            value = jnp.take_along_axis(table, jnp.where(inside, index - first, 0), axis=1)
            found = jnp.where(inside, value, found)
        weight_ref[:, start:start + LANES] = found
    total = jnp.zeros((size, size), F32)
    for level in range(1, dist):
        total = total + qb_ref[level - 1] * row(size, -(dist - level) * size, -beta)
    branch_ref[...] = jnp.sum(total, axis=1, keepdims=True)


def main_kernel(dist, live_ref, qm_ref, *refs):
    rights = refs[:dist - 1]
    weight_ref, branch_ref, own_ref, end_ref, pair_ref, qm1_ref, out_ref = refs[dist - 1:]
    size = weight_ref.shape[0]
    beta = 1.0 / (dist * size)

    @pl.when(live_ref[0] == 0)
    def _():
        for ref in (pair_ref, qm1_ref, out_ref):
            ref[...] = jnp.zeros_like(ref)

    @pl.when(live_ref[0] != 0)
    def _():
        summed = jnp.zeros((size, size), F32)
        tail = jnp.zeros((1, size), F32)
        for shift in range(1, dist):
            right = rights[shift - 1][...]
            summed = summed + product(qm_ref[shift - 1], right)
            tail = tail + jnp.sum(right * column(size, shift * size, beta), axis=0, keepdims=True)
        rows = lax.broadcasted_iota(jnp.int32, (size, size), 0)
        columns = lax.broadcasted_iota(jnp.int32, (size, size), 1)
        upper = jnp.where(rows <= columns, 1.0, 0.0).astype(BF16)
        own = jnp.sum(jnp.where(rows == columns, own_ref[...], 0), axis=1, keepdims=True)
        both = own + end_ref[...]
        allowed = (both == 3) | (both == 5)
        pair = jnp.where(allowed, weight_ref[...] * (1.0 + 0.8 * summed), 0.0)
        pair_ref[...] = pair
        high, low = halves(pair * row(size, 0, -beta))
        branch = (branch_ref[...] + (dot(high, upper) + dot(low, upper))) * (row(size, 0, beta) * beta)
        qm1_ref[...] = branch
        high, low = halves(branch * column(size, 0, beta))
        start = tail + (dot(upper, high) + dot(upper, low))
        out_ref[...] = summed + start * (0.01 * column(size, 0, -beta))


def shifted(block, distance, width):
    return lax.ppermute(block, "row", [(i + distance, i) for i in range(width - distance)])


def per_device(qm, qm1, qb, codes, energy_index, turner):
    width = lax.axis_size("row")
    dist, size = qm.shape[2] + 1, qm.shape[3]
    live = (lax.axis_index("row") + dist < width).astype(jnp.int32).reshape(1)
    lives = width - dist
    rights = [
        lax.ppermute(qm1[0, 0, dist - shift - 1], "row", [(i + shift, i) for i in range(lives)])
        for shift in range(1, dist)
    ]
    own = codes[0]
    end = lax.ppermute(own, "row", [(i + dist, i) for i in range(lives)])
    vmem = pl.BlockSpec(memory_space=pltpu.VMEM)
    smem = pl.BlockSpec(memory_space=pltpu.SMEM)
    square = jax.ShapeDtypeStruct((size, size), F32)
    weight, branch = pl.pallas_call(
        functools.partial(weights_kernel, dist),
        out_shape=(square, jax.ShapeDtypeStruct((size, 1), F32)),
        in_specs=[vmem] * 3,
        out_specs=[vmem] * 2,
        compiler_params=pltpu.CompilerParams(vmem_limit_bytes=16 << 20),
        cost_estimate=pl.CostEstimate(flops=40 * size * size, bytes_accessed=4 * size * size * (dist + 1), transcendentals=0),
        name="weights",
    )(energy_index[0, 0], jnp.pad(turner, (0, -turner.shape[0] % LANES))[None], qb[0, 0])
    pair, branch, out = pl.pallas_call(
        functools.partial(main_kernel, dist),
        out_shape=(square,) * 3,
        in_specs=[smem] + [vmem] * (dist + 4),
        out_specs=[vmem] * 3,
        compiler_params=pltpu.CompilerParams(vmem_limit_bytes=32 << 20),
        name="blocks",
    )(live, qm[0, 0], *rights, weight, branch, own, end)
    return pair[None, None], branch[None, None], out[None, None]


def solution(mesh):
    blocks = P("seq", "row", None, None, None)
    return jax.shard_map(
        per_device,
        mesh=mesh,
        in_specs=(blocks, blocks, blocks, P("seq", "row", None), P("seq", "row", None, None), P()),
        out_specs=(P("seq", "row", None, None),) * 3,
        check_vma=False,
    )
```

```python
import functools

import jax
import jax.numpy as jnp
import numpy as np
from jax import lax
from jax.experimental import pallas as pl
from jax.experimental.pallas import tpu as pltpu
from jax.sharding import PartitionSpec as P

F32 = jnp.float32
BF16 = jnp.bfloat16
LANES = 128
FIRST = 1
LATE = 4
GATE = 1
PLAN = (
    (5, (5, 6, 7), (0, 4, 2, 3, -1, 1, 0)),
    (3, (3, 4, 5), (1, 4, -1, 1, 0, 2, 3)),
    (5, (5, 6, 7), (0, 2, 4, 3, -1, 1, 0)),
    (3, (3, 4, 5), (4, 2, -1, 1, 0, 3, 1)),
    (4, (4, 5, 7), (1, 0, 3, -1, 2, 4, 0)),
    (4, (3, 4, 7), (1, 0, 2, -1, 3, 4, 0)),
    (5, (3, 6, 7), (1, 0, 1, 2, 3, 2, 0)),
    (3, (3, 4, 6), (1, 0, -1, 1, 4, 2, 2)),
)


def colored(flows):
    count = max(max(np.bincount([f[end] for f in flows])) for end in (0, 1))
    used = {}
    rounds = []
    for number, (source, target) in enumerate(flows):
        free = [[c for c in range(count) if (end, at, c) not in used] for end, at in ((0, source), (1, target))]
        common = [c for c in free[0] if c in free[1]]
        rounds.append(common[0] if common else free[0][0])
        if not common:
            first, second = free[0][0], free[1][0]
            chain, end, at, want = [], 1, target, first
            while (end, at, want) in used:
                other = used[end, at, want]
                chain.append(other)
                end, at = 1 - end, flows[other][1 - end]
                want = first + second - want
            for other in chain:
                for side in (0, 1):
                    del used[side, flows[other][side], rounds[other]]
            for other in chain:
                rounds[other] = first + second - rounds[other]
                for side in (0, 1):
                    used[side, flows[other][side], rounds[other]] = other
        for side in (0, 1):
            used[side, flows[number][side], rounds[number]] = number
    return rounds, count


class Plan:
    def __init__(self, width, dist):
        self.lives = lives = max(width - dist, 0)
        far = {}
        routes = {}
        for i in range(lives):
            offset, products, hints = PLAN[i % len(PLAN)]
            if i + offset < width and max(products) < dist:
                far[i] = (i + offset, products)
            for m in range(1, dist):
                at = far[i][0] if i in far and m in far[i][1] else i
                if at != i + m:
                    routes.setdefault((i + m, at), []).append((at == i, i, m, hints[m - 1] if m <= len(hints) else -1))
        rounds = {route: blocks[0][3] for route, blocks in routes.items()}
        ends = [(side, route[side], t) for route, t in rounds.items() for side in (0, 1)]
        if len(set(ends)) < len(ends) or min(rounds.values(), default=0) < 0:
            order = sorted(routes, key=lambda route: -len(routes[route]))
            rounds = dict(zip(order, colored(order)[0]))
        self.rounds = max(rounds.values(), default=-1) + 1
        self.pairs = [[route for route in routes if rounds[route] == t] for t in range(self.rounds)]
        self.sizes = [max(len(routes[route]) for route in pairs) for pairs in self.pairs]
        self.slots = slots = max([len(products) for _, products in far.values()], default=0)
        starts = np.concatenate([[0], np.cumsum(self.sizes)]).astype(int)
        self.send = np.full((starts[-1], width), -1, np.int32)
        self.near = np.full((starts[-1], width), -1, np.int32)
        far_slot = np.full((starts[-1], width), -1, np.int32)
        for (source, target), blocks in routes.items():
            for line, (is_near, i, m, _) in enumerate(sorted(blocks), starts[rounds[source, target]]):
                self.send[line, source] = dist - 1 - m
                if is_near:
                    self.near[line, target] = m
                else:
                    far_slot[line, target] = far[i][1].index(m)
        self.starts = starts
        self.places = [(t, at) for t, count in enumerate(self.sizes) for at in range(count)]
        lines = [line for line in range(starts[-1]) if far_slot[line].max() >= 0]
        self.far_rounds = sorted({self.places[line][0] for line in lines})
        self.far_places = [(self.far_rounds.index(t), at) for t, at in (self.places[line] for line in lines)]
        self.moved = np.full((slots, width), -1, np.int32)
        far_m = np.full((slots, width), -1, np.int32)
        own = np.full((1, width), -1, np.int32)
        for i, (at, products) in far.items():
            self.moved[:len(products), i] = np.array(products) - 1
            far_m[:len(products), at] = products
            if at - i in products:
                own[0, at] = products.index(at - i)
        self.far = np.concatenate([far_m, far_slot[lines], own])
        self.there = [(i, at) for i, (at, _) in far.items()]
        self.back = [(at, i) for i, at in self.there]


def halves(x):
    high = x.astype(BF16)
    return high, (x - high.astype(F32)).astype(BF16)


def dot(a, b):
    return jnp.dot(a, b, preferred_element_type=F32)


def product(left, right):
    left_high, left_low = halves(left)
    right_high, right_low = halves(right)
    return dot(left_high, right_high) + dot(left_high, right_low) + dot(left_low, right_high)


def column(size, start, beta):
    steps = lax.broadcasted_iota(jnp.int32, (size, 1), 0) + start
    return jnp.exp(steps.astype(F32) * -beta)


def row(size, start, beta):
    steps = lax.broadcasted_iota(jnp.int32, (1, size), 1) + start
    return jnp.exp(steps.astype(F32) * -beta)


def weights_kernel(dist, index_ref, turner_ref, qb_ref, weight_ref, branch_ref):
    size = index_ref.shape[0]
    beta = 1.0 / (dist * size)
    entries = turner_ref.shape[1]
    for start in range(0, size, LANES):
        index = index_ref[:, start:start + LANES]
        found = jnp.zeros(index.shape, F32)
        for first in range(0, entries, LANES):
            table = jnp.exp(-turner_ref[:, first:first + LANES])
            table = jnp.broadcast_to(table, index.shape)
            inside = (index >= first) & (index < first + LANES)
            value = jnp.take_along_axis(table, jnp.where(inside, index - first, 0), axis=1)
            found = jnp.where(inside, value, found)
        weight_ref[:, start:start + LANES] = found
    total = jnp.zeros((size, size), F32)
    for level in range(1, dist):
        total = total + qb_ref[level - 1] * row(size, -(dist - level) * size, -beta)
    branch_ref[...] = jnp.sum(total, axis=1, keepdims=True)


def looked_up(table, me):
    entries = []
    for first in range(0, len(table), 7):
        lines = table[first:first + 7].astype(np.int64) + 1
        words = sum(line << (4 * at) for at, line in enumerate(lines))
        word = jnp.int32(0)
        for column, value in enumerate(words):
            word = jnp.where(me == column, jnp.int32(value), word)
        entries += [((word >> (4 * at)) & 15) - 1 for at in range(len(lines))]
    return entries


def pick_kernel(tables, *refs):
    me = lax.axis_index("row")
    sems = refs[-1]
    operands, places = refs[:len(tables)], refs[len(tables):-1]
    places = [ref.at[slot] for ref in places for slot in range(ref.shape[0])]
    copies = []
    for table, operand in zip(tables, operands):
        for entry in looked_up(table, me):
            number = len(copies)
            copy = pltpu.make_async_copy(operand.at[jnp.maximum(entry, 0)], places[number], sems.at[number])
            copies.append((entry >= 0, copy))
    for wanted, copy in copies:
        pl.when(wanted)(copy.start)
    for wanted, copy in copies:
        pl.when(wanted)(copy.wait)


def far_kernel(plan, dist, table_ref, qm1_ref, left_ref, *refs):
    me = lax.axis_index("row")
    rights, out_ref = refs[:-1], refs[-1]
    size = out_ref.shape[1]
    beta = 1.0 / (dist * size)
    out_ref[...] = jnp.zeros_like(out_ref)
    blocks = [rights[t].at[at] for t, at in plan.far_places]
    for number, right_ref in enumerate(blocks + [None]):
        slot = table_ref[plan.slots + number, me]

        @pl.when(slot >= 0)
        def _():
            m = table_ref[jnp.maximum(slot, 0), me]
            right = right_ref[...] if right_ref is not None else qm1_ref[dist - 1 - m]
            out_ref[:size] += product(left_ref[jnp.maximum(slot, 0)], right)
            out_ref[size:size + 1] += jnp.sum(right * column(size, m * size, beta), axis=0, keepdims=True)


def near_kernel(plan, dist, table_ref, qm_ref, *refs):
    me = lax.axis_index("row")
    rights, out_ref = refs[:-1], refs[-1]
    size = out_ref.shape[1]
    beta = 1.0 / (dist * size)
    out_ref[...] = jnp.zeros_like(out_ref)
    for number, (t, at) in enumerate(plan.places):
        right_ref = rights[t].at[at]
        m = table_ref[number, me]

        @pl.when(m >= 0)
        def _():
            right = right_ref[...]
            out_ref[:size] += product(qm_ref[m - 1], right)
            out_ref[size:size + 1] += jnp.sum(right * column(size, m * size, beta), axis=0, keepdims=True)


def last_kernel(plan, dist, near_ref, far_ref, weight_ref, branch_ref, own_ref, end_ref, pair_ref, qm1_ref, out_ref):
    live = lax.axis_index("row") < plan.lives
    size = weight_ref.shape[0]
    beta = 1.0 / (dist * size)

    @pl.when(jnp.logical_not(live))
    def _():
        for ref in (pair_ref, qm1_ref, out_ref):
            ref[...] = jnp.zeros_like(ref)

    @pl.when(live)
    def _():
        summed = near_ref[:size] + far_ref[:size]
        tail = near_ref[size:size + 1] + far_ref[size:size + 1]
        rows = lax.broadcasted_iota(jnp.int32, (size, size), 0)
        columns = lax.broadcasted_iota(jnp.int32, (size, size), 1)
        upper = jnp.where(rows <= columns, 1.0, 0.0).astype(BF16)
        own = jnp.sum(jnp.where(rows == columns, own_ref[...], 0), axis=1, keepdims=True)
        both = own + end_ref[...]
        allowed = (both == 3) | (both == 5)
        pair = jnp.where(allowed, weight_ref[...] * (1.0 + 0.8 * summed), 0.0)
        pair_ref[...] = pair
        high, low = halves(pair * row(size, 0, -beta))
        branch = (branch_ref[...] + (dot(high, upper) + dot(low, upper))) * (row(size, 0, beta) * beta)
        qm1_ref[...] = branch
        high, low = halves(branch * column(size, 0, beta))
        start = tail + (dot(upper, high) + dot(upper, low))
        out_ref[...] = summed + start * (0.01 * column(size, 0, -beta))


def per_device(qm, qm1, qb, codes, energy_index, turner):
    width = lax.axis_size("row")
    dist, size = qm.shape[2] + 1, qm.shape[3]
    plan = Plan(width, dist)
    qm, qm1, qb, index = qm[0, 0], qm1[0, 0], qb[0, 0], energy_index[0, 0]
    vmem = pl.BlockSpec(memory_space=pltpu.VMEM)
    smem = pl.BlockSpec(memory_space=pltpu.SMEM)
    hbm = pl.BlockSpec(memory_space=pltpu.HBM)
    square = jax.ShapeDtypeStruct((size, size), F32)
    tall = jax.ShapeDtypeStruct((size + 8, size), F32)

    def call(kernel, name, outs, ins, args, products, scratch=(), vmem_mib=40):
        many = isinstance(outs, tuple)
        return pl.pallas_call(
            kernel,
            out_shape=outs,
            in_specs=ins,
            out_specs=(vmem,) * len(outs) if many else vmem,
            scratch_shapes=scratch,
            compiler_params=pltpu.CompilerParams(vmem_limit_bytes=vmem_mib << 20),
            cost_estimate=pl.CostEstimate(
                flops=products * 6 * size**3, bytes_accessed=4 * size * size * (dist + 1), transcendentals=0
            ),
            name=name,
        )(*args)

    rounds = plan.rounds
    first = min(FIRST, rounds)
    stack = [jax.ShapeDtypeStruct((count, size, size), F32) for count in [plan.slots] + plan.sizes]
    cut = plan.starts[first]

    def pick(name, operands, tables, outs):
        lines = sum(len(table) for table in tables)
        return call(
            functools.partial(pick_kernel, tables), name, outs, [hbm] * len(operands), operands, 0,
            [pltpu.SemaphoreType.DMA((lines,))], 60,
        )

    picked = pick("pick_first", (qm, qm1), (plan.moved, plan.send[:cut]), tuple(stack[:first + 1]))
    left, blocks = picked[0], picked[1:]
    blocks += pick("pick_rest", (qm1,), (plan.send[cut:],), tuple(stack[first + 1:]))
    left = lax.ppermute(left, "row", plan.there)
    early = [t for t in range(rounds) if t < LATE or t in plan.far_rounds]
    late = [t for t in range(rounds) if t not in early]
    rights = {t: lax.ppermute(blocks[t], "row", plan.pairs[t]) for t in early}
    own = codes[0]
    end = lax.ppermute(own, "row", [(i + dist, i) for i in range(plan.lives)])
    weight, branch = call(
        functools.partial(weights_kernel, dist), "weights", (square, jax.ShapeDtypeStruct((size, 1), F32)), [vmem] * 3,
        (index, jnp.pad(turner, (0, -turner.shape[0] % LANES))[None], qb), 0,
    )
    far = call(
        functools.partial(far_kernel, plan, dist), "far", tall, [smem] + [vmem] * (2 + len(plan.far_rounds)),
        (jnp.asarray(plan.far), qm1, left, *(rights[t] for t in plan.far_rounds)), 3,
    )
    if late and GATE:
        held, far = lax.optimization_barrier(([blocks[t] for t in late], far))
    else:
        held = [blocks[t] for t in late]
    far = lax.ppermute(far, "row", plan.back)
    rights.update((t, lax.ppermute(block, "row", plan.pairs[t])) for t, block in zip(late, held))
    near = call(
        functools.partial(near_kernel, plan, dist), "near", tall, [smem] + [vmem] * (1 + rounds),
        (jnp.asarray(plan.near), qm, *(rights[t] for t in range(rounds))), 7,
    )
    pair, branch, out = call(
        functools.partial(last_kernel, plan, dist), "last", (square,) * 3, [vmem] * 6,
        (near, far, weight, branch, own, end), 2,
    )
    return pair[None, None], branch[None, None], out[None, None]


def solution(mesh):
    blocks = P("seq", "row", None, None, None)
    return jax.shard_map(
        per_device,
        mesh=mesh,
        in_specs=(blocks, blocks, blocks, P("seq", "row", None), P("seq", "row", None, None), P()),
        out_specs=(P("seq", "row", None, None),) * 3,
        check_vma=False,
    )
```

```python
import functools

import jax
import jax.numpy as jnp
import numpy as np
from jax import lax
from jax.experimental import pallas as pl
from jax.experimental.pallas import tpu as pltpu
from jax.sharding import PartitionSpec as P

F32 = jnp.float32
BF16 = jnp.bfloat16
LANES = 128
FIRST = 1
LATE = 4
PLAN = (
    (5, (5, 6, 7), (4, 1, 2, 3, -1, 1, 0)),
    (3, (3, 4, 5), (4, 0, -1, 1, 0, 2, 3)),
    (5, (5, 6, 7), (1, 0, 2, 3, -1, 1, 0)),
    (3, (3, 4, 5), (2, 3, -1, 1, 0, 4, 1)),
    (4, (4, 5, 7), (1, 0, 3, -1, 2, 4, 1)),
    (4, (3, 4, 7), (1, 0, 2, -1, 3, 4, 1)),
    (5, (3, 6, 7), (1, 0, 1, 2, 3, 0, 2)),
    (3, (3, 4, 6), (1, 0, -1, 2, 4, 0, 2)),
)


def colored(flows):
    count = max(max(np.bincount([f[end] for f in flows])) for end in (0, 1))
    used = {}
    rounds = []
    for number, (source, target) in enumerate(flows):
        free = [[c for c in range(count) if (end, at, c) not in used] for end, at in ((0, source), (1, target))]
        common = [c for c in free[0] if c in free[1]]
        rounds.append(common[0] if common else free[0][0])
        if not common:
            first, second = free[0][0], free[1][0]
            chain, end, at, want = [], 1, target, first
            while (end, at, want) in used:
                other = used[end, at, want]
                chain.append(other)
                end, at = 1 - end, flows[other][1 - end]
                want = first + second - want
            for other in chain:
                for side in (0, 1):
                    del used[side, flows[other][side], rounds[other]]
            for other in chain:
                rounds[other] = first + second - rounds[other]
                for side in (0, 1):
                    used[side, flows[other][side], rounds[other]] = other
        for side in (0, 1):
            used[side, flows[number][side], rounds[number]] = number
    return rounds, count


class Plan:
    def __init__(self, width, dist):
        self.lives = lives = max(width - dist, 0)
        far = {}
        routes = {}
        for i in range(lives):
            offset, products, hints = PLAN[i % len(PLAN)]
            if i + offset < width and max(products) < dist:
                far[i] = (i + offset, products)
            for m in range(1, dist):
                at = far[i][0] if i in far and m in far[i][1] else i
                if at != i + m:
                    routes.setdefault((i + m, at), []).append((at == i, i, m, hints[m - 1] if m <= len(hints) else -1))
        rounds = {route: blocks[0][3] for route, blocks in routes.items()}
        ends = [(side, route[side], t) for route, t in rounds.items() for side in (0, 1)]
        if len(set(ends)) < len(ends) or min(rounds.values(), default=0) < 0:
            order = sorted(routes, key=lambda route: -len(routes[route]))
            rounds = dict(zip(order, colored(order)[0]))
        self.rounds = max(rounds.values(), default=-1) + 1
        self.pairs = [[route for route in routes if rounds[route] == t] for t in range(self.rounds)]
        self.sizes = [max(len(routes[route]) for route in pairs) for pairs in self.pairs]
        self.slots = slots = max([len(products) for _, products in far.values()], default=0)
        starts = np.concatenate([[0], np.cumsum(self.sizes)]).astype(int)
        self.send = np.full((starts[-1], width), -1, np.int32)
        self.near = np.full((starts[-1], width), -1, np.int32)
        far_slot = np.full((starts[-1], width), -1, np.int32)
        for (source, target), blocks in routes.items():
            for line, (is_near, i, m, _) in enumerate(sorted(blocks), starts[rounds[source, target]]):
                self.send[line, source] = dist - 1 - m
                if is_near:
                    self.near[line, target] = m
                else:
                    far_slot[line, target] = far[i][1].index(m)
        self.starts = starts
        self.places = [(t, at) for t, count in enumerate(self.sizes) for at in range(count)]
        lines = [line for line in range(starts[-1]) if far_slot[line].max() >= 0]
        self.far_rounds = sorted({self.places[line][0] for line in lines})
        self.far_places = [(self.far_rounds.index(t), at) for t, at in (self.places[line] for line in lines)]
        self.moved = np.full((slots, width), -1, np.int32)
        far_m = np.full((slots, width), -1, np.int32)
        own = np.full((1, width), -1, np.int32)
        for i, (at, products) in far.items():
            self.moved[:len(products), i] = np.array(products) - 1
            far_m[:len(products), at] = products
            if at - i in products:
                own[0, at] = products.index(at - i)
        self.far = np.concatenate([far_m, far_slot[lines], own])
        self.there = [(i, at) for i, (at, _) in far.items()]
        self.back = [(at, i) for i, at in self.there]


def halves(x):
    high = x.astype(BF16)
    return high, (x - high.astype(F32)).astype(BF16)


def dot(a, b):
    return jnp.dot(a, b, preferred_element_type=F32)


def product(left, right):
    left_high, left_low = halves(left)
    right_high, right_low = halves(right)
    return dot(left_high, right_high) + dot(left_high, right_low) + dot(left_low, right_high)


def column(size, start, beta):
    steps = lax.broadcasted_iota(jnp.int32, (size, 1), 0) + start
    return jnp.exp(steps.astype(F32) * -beta)


def row(size, start, beta):
    steps = lax.broadcasted_iota(jnp.int32, (1, size), 1) + start
    return jnp.exp(steps.astype(F32) * -beta)


def weights_kernel(dist, index_ref, turner_ref, qb_ref, weight_ref, branch_ref):
    size = index_ref.shape[0]
    beta = 1.0 / (dist * size)
    entries = turner_ref.shape[1]
    for start in range(0, size, LANES):
        index = index_ref[:, start:start + LANES]
        found = jnp.zeros(index.shape, F32)
        for first in range(0, entries, LANES):
            table = jnp.exp(-turner_ref[:, first:first + LANES])
            table = jnp.broadcast_to(table, index.shape)
            inside = (index >= first) & (index < first + LANES)
            value = jnp.take_along_axis(table, jnp.where(inside, index - first, 0), axis=1)
            found = jnp.where(inside, value, found)
        weight_ref[:, start:start + LANES] = found
    total = jnp.zeros((size, size), F32)
    for level in range(1, dist):
        total = total + qb_ref[level - 1] * row(size, -(dist - level) * size, -beta)
    branch_ref[...] = jnp.sum(total, axis=1, keepdims=True)


def looked_up(table, me):
    entries = []
    for first in range(0, len(table), 7):
        lines = table[first:first + 7].astype(np.int64) + 1
        words = sum(line << (4 * at) for at, line in enumerate(lines))
        word = jnp.int32(0)
        for column, value in enumerate(words):
            word = jnp.where(me == column, jnp.int32(value), word)
        entries += [((word >> (4 * at)) & 15) - 1 for at in range(len(lines))]
    return entries


def pick_kernel(tables, *refs):
    me = lax.axis_index("row")
    sems = refs[-1]
    operands, places = refs[:len(tables)], refs[len(tables):-1]
    places = [ref.at[slot] for ref in places for slot in range(ref.shape[0])]
    copies = []
    for table, operand in zip(tables, operands):
        for entry in looked_up(table, me):
            number = len(copies)
            copy = pltpu.make_async_copy(operand.at[jnp.maximum(entry, 0)], places[number], sems.at[number])
            copies.append((entry >= 0, copy))
    for wanted, copy in copies:
        pl.when(wanted)(copy.start)
    for wanted, copy in copies:
        pl.when(wanted)(copy.wait)


def far_kernel(plan, dist, table_ref, qm1_ref, left_ref, *refs):
    me = lax.axis_index("row")
    rights, out_ref = refs[:-1], refs[-1]
    size = out_ref.shape[1]
    beta = 1.0 / (dist * size)
    out_ref[...] = jnp.zeros_like(out_ref)
    blocks = [rights[t].at[at] for t, at in plan.far_places]
    for number, right_ref in enumerate(blocks + [None]):
        slot = table_ref[plan.slots + number, me]

        @pl.when(slot >= 0)
        def _():
            m = table_ref[jnp.maximum(slot, 0), me]
            right = right_ref[...] if right_ref is not None else qm1_ref[dist - 1 - m]
            out_ref[:size] += product(left_ref[jnp.maximum(slot, 0)], right)
            out_ref[size:size + 1] += jnp.sum(right * column(size, m * size, beta), axis=0, keepdims=True)


def near_kernel(plan, dist, table_ref, qm_ref, *refs):
    me = lax.axis_index("row")
    rights, out_ref = refs[:-1], refs[-1]
    size = out_ref.shape[1]
    beta = 1.0 / (dist * size)
    out_ref[...] = jnp.zeros_like(out_ref)
    for number, (t, at) in enumerate(plan.places):
        right_ref = rights[t].at[at]
        m = table_ref[number, me]

        @pl.when(m >= 0)
        def _():
            right = right_ref[...]
            out_ref[:size] += product(qm_ref[m - 1], right)
            out_ref[size:size + 1] += jnp.sum(right * column(size, m * size, beta), axis=0, keepdims=True)


def last_kernel(plan, dist, near_ref, far_ref, weight_ref, branch_ref, own_ref, end_ref, pair_ref, qm1_ref, out_ref):
    live = lax.axis_index("row") < plan.lives
    size = weight_ref.shape[0]
    beta = 1.0 / (dist * size)

    @pl.when(jnp.logical_not(live))
    def _():
        for ref in (pair_ref, qm1_ref, out_ref):
            ref[...] = jnp.zeros_like(ref)

    @pl.when(live)
    def _():
        summed = near_ref[:size] + far_ref[:size]
        tail = near_ref[size:size + 1] + far_ref[size:size + 1]
        rows = lax.broadcasted_iota(jnp.int32, (size, size), 0)
        columns = lax.broadcasted_iota(jnp.int32, (size, size), 1)
        upper = jnp.where(rows <= columns, 1.0, 0.0).astype(BF16)
        own = jnp.sum(jnp.where(rows == columns, own_ref[...], 0), axis=1, keepdims=True)
        both = own + end_ref[...]
        allowed = (both == 3) | (both == 5)
        pair = jnp.where(allowed, weight_ref[...] * (1.0 + 0.8 * summed), 0.0)
        pair_ref[...] = pair
        high, low = halves(pair * row(size, 0, -beta))
        branch = (branch_ref[...] + (dot(high, upper) + dot(low, upper))) * (row(size, 0, beta) * beta)
        qm1_ref[...] = branch
        high, low = halves(branch * column(size, 0, beta))
        start = tail + (dot(upper, high) + dot(upper, low))
        out_ref[...] = summed + start * (0.01 * column(size, 0, -beta))


def per_device(qm, qm1, qb, codes, energy_index, turner):
    width = lax.axis_size("row")
    dist, size = qm.shape[2] + 1, qm.shape[3]
    plan = Plan(width, dist)
    qm, qm1, qb, index = qm[0, 0], qm1[0, 0], qb[0, 0], energy_index[0, 0]
    vmem = pl.BlockSpec(memory_space=pltpu.VMEM)
    smem = pl.BlockSpec(memory_space=pltpu.SMEM)
    hbm = pl.BlockSpec(memory_space=pltpu.HBM)
    square = jax.ShapeDtypeStruct((size, size), F32)
    tall = jax.ShapeDtypeStruct((size + 8, size), F32)

    def call(kernel, name, outs, ins, args, products, scratch=(), vmem_mib=40):
        many = isinstance(outs, tuple)
        return pl.pallas_call(
            kernel,
            out_shape=outs,
            in_specs=ins,
            out_specs=(vmem,) * len(outs) if many else vmem,
            scratch_shapes=scratch,
            compiler_params=pltpu.CompilerParams(vmem_limit_bytes=vmem_mib << 20),
            cost_estimate=pl.CostEstimate(
                flops=products * 6 * size**3, bytes_accessed=4 * size * size * (dist + 1), transcendentals=0
            ),
            name=name,
        )(*args)

    rounds = plan.rounds
    first = min(FIRST, rounds)
    stack = [jax.ShapeDtypeStruct((count, size, size), F32) for count in [plan.slots] + plan.sizes]
    cut = plan.starts[first]

    def pick(name, operands, tables, outs):
        lines = sum(len(table) for table in tables)
        return call(
            functools.partial(pick_kernel, tables), name, outs, [hbm] * len(operands), operands, 0,
            [pltpu.SemaphoreType.DMA((lines,))], 60,
        )

    picked = pick("pick_first", (qm, qm1), (plan.moved, plan.send[:cut]), tuple(stack[:first + 1]))
    left, blocks = picked[0], picked[1:]
    mid = min(LATE, rounds)
    end = plan.starts[mid]
    blocks += pick("pick_rest", (qm1,), (plan.send[cut:end],), tuple(stack[first + 1:mid + 1]))
    if rounds > mid:
        blocks += pick("pick_late", (qm1,), (plan.send[end:],), tuple(stack[mid + 1:]))
    left = lax.ppermute(left, "row", plan.there)
    early = [t for t in range(rounds) if t < LATE or t in plan.far_rounds]
    late = [t for t in range(rounds) if t not in early]
    rights = {t: lax.ppermute(blocks[t], "row", plan.pairs[t]) for t in early}
    own = codes[0]
    end = lax.ppermute(own, "row", [(i + dist, i) for i in range(plan.lives)])
    weight, branch = call(
        functools.partial(weights_kernel, dist), "weights", (square, jax.ShapeDtypeStruct((size, 1), F32)), [vmem] * 3,
        (index, jnp.pad(turner, (0, -turner.shape[0] % LANES))[None], qb), 0,
    )
    far = call(
        functools.partial(far_kernel, plan, dist), "far", tall, [smem] + [vmem] * (2 + len(plan.far_rounds)),
        (jnp.asarray(plan.far), qm1, left, *(rights[t] for t in plan.far_rounds)), 3,
    )
    if late:
        held, far = lax.optimization_barrier(([blocks[t] for t in late], far))
    else:
        held = [blocks[t] for t in late]
    far = lax.ppermute(far, "row", plan.back)
    rights.update((t, lax.ppermute(block, "row", plan.pairs[t])) for t, block in zip(late, held))
    near = call(
        functools.partial(near_kernel, plan, dist), "near", tall, [smem] + [vmem] * (1 + rounds),
        (jnp.asarray(plan.near), qm, *(rights[t] for t in range(rounds))), 7,
    )
    pair, branch, out = call(
        functools.partial(last_kernel, plan, dist), "last", (square,) * 3, [vmem] * 6,
        (near, far, weight, branch, own, end), 2,
    )
    return pair[None, None], branch[None, None], out[None, None]


def solution(mesh):
    blocks = P("seq", "row", None, None, None)
    return jax.shard_map(
        per_device,
        mesh=mesh,
        in_specs=(blocks, blocks, blocks, P("seq", "row", None), P("seq", "row", None, None), P()),
        out_specs=(P("seq", "row", None, None),) * 3,
        check_vma=False,
    )
```

```python
import functools

import jax
import jax.numpy as jnp
import numpy as np
from jax import lax
from jax.experimental import pallas as pl
from jax.experimental.pallas import tpu as pltpu
from jax.sharding import PartitionSpec as P

F32 = jnp.float32
BF16 = jnp.bfloat16
LANES = 128
FIRST = 1
LATE = 4
PLAN = (
    (5, (5, 6, 7), (4, 1, 2, 3, -1, 1, 0)),
    (3, (3, 4, 5), (4, 0, -1, 1, 0, 2, 3)),
    (5, (5, 6, 7), (1, 0, 2, 3, -1, 1, 0)),
    (3, (3, 4, 5), (2, 3, -1, 1, 0, 4, 1)),
    (4, (4, 5, 7), (1, 0, 3, -1, 2, 4, 1)),
    (4, (3, 4, 7), (1, 0, 2, -1, 3, 4, 1)),
    (5, (3, 6, 7), (1, 0, 1, 2, 3, 0, 2)),
    (3, (3, 4, 6), (1, 0, -1, 2, 4, 0, 2)),
)


def colored(flows):
    count = max(max(np.bincount([f[end] for f in flows])) for end in (0, 1))
    used = {}
    rounds = []
    for number, (source, target) in enumerate(flows):
        free = [[c for c in range(count) if (end, at, c) not in used] for end, at in ((0, source), (1, target))]
        common = [c for c in free[0] if c in free[1]]
        rounds.append(common[0] if common else free[0][0])
        if not common:
            first, second = free[0][0], free[1][0]
            chain, end, at, want = [], 1, target, first
            while (end, at, want) in used:
                other = used[end, at, want]
                chain.append(other)
                end, at = 1 - end, flows[other][1 - end]
                want = first + second - want
            for other in chain:
                for side in (0, 1):
                    del used[side, flows[other][side], rounds[other]]
            for other in chain:
                rounds[other] = first + second - rounds[other]
                for side in (0, 1):
                    used[side, flows[other][side], rounds[other]] = other
        for side in (0, 1):
            used[side, flows[number][side], rounds[number]] = number
    return rounds, count


class Plan:
    def __init__(self, width, dist):
        self.lives = lives = max(width - dist, 0)
        far = {}
        routes = {}
        for i in range(lives):
            offset, products, hints = PLAN[i % len(PLAN)]
            if i + offset < width and max(products) < dist:
                far[i] = (i + offset, products)
            for m in range(1, dist):
                at = far[i][0] if i in far and m in far[i][1] else i
                if at != i + m:
                    routes.setdefault((i + m, at), []).append((at == i, i, m, hints[m - 1] if m <= len(hints) else -1))
        rounds = {route: blocks[0][3] for route, blocks in routes.items()}
        ends = [(side, route[side], t) for route, t in rounds.items() for side in (0, 1)]
        if len(set(ends)) < len(ends) or min(rounds.values(), default=0) < 0:
            order = sorted(routes, key=lambda route: -len(routes[route]))
            rounds = dict(zip(order, colored(order)[0]))
        self.rounds = max(rounds.values(), default=-1) + 1
        self.pairs = [[route for route in routes if rounds[route] == t] for t in range(self.rounds)]
        self.sizes = [max(len(routes[route]) for route in pairs) for pairs in self.pairs]
        self.slots = slots = max([len(products) for _, products in far.values()], default=0)
        starts = np.concatenate([[0], np.cumsum(self.sizes)]).astype(int)
        self.send = np.full((starts[-1], width), -1, np.int32)
        self.near = np.full((starts[-1], width), -1, np.int32)
        far_slot = np.full((starts[-1], width), -1, np.int32)
        for (source, target), blocks in routes.items():
            for line, (is_near, i, m, _) in enumerate(sorted(blocks), starts[rounds[source, target]]):
                self.send[line, source] = dist - 1 - m
                if is_near:
                    self.near[line, target] = m
                else:
                    far_slot[line, target] = far[i][1].index(m)
        self.starts = starts
        self.places = [(t, at) for t, count in enumerate(self.sizes) for at in range(count)]
        lines = [line for line in range(starts[-1]) if far_slot[line].max() >= 0]
        self.far_rounds = sorted({self.places[line][0] for line in lines})
        self.far_places = [(self.far_rounds.index(t), at) for t, at in (self.places[line] for line in lines)]
        self.moved = np.full((slots, width), -1, np.int32)
        far_m = np.full((slots, width), -1, np.int32)
        own = np.full((1, width), -1, np.int32)
        for i, (at, products) in far.items():
            self.moved[:len(products), i] = np.array(products) - 1
            far_m[:len(products), at] = products
            if at - i in products:
                own[0, at] = products.index(at - i)
        self.far = np.concatenate([far_m, far_slot[lines], own])
        self.there = [(i, at) for i, (at, _) in far.items()]
        self.back = [(at, i) for i, at in self.there]


def halves(x):
    high = x.astype(BF16)
    return high, (x - high.astype(F32)).astype(BF16)


def dot(a, b):
    return jnp.dot(a, b, preferred_element_type=F32)


def product(left, right):
    left_high, left_low = halves(left)
    right_high, right_low = halves(right)
    return dot(left_high, right_high) + dot(left_high, right_low) + dot(left_low, right_high)


def column(size, start, beta):
    steps = lax.broadcasted_iota(jnp.int32, (size, 1), 0) + start
    return jnp.exp(steps.astype(F32) * -beta)


def row(size, start, beta):
    steps = lax.broadcasted_iota(jnp.int32, (1, size), 1) + start
    return jnp.exp(steps.astype(F32) * -beta)


def weights_kernel(dist, index_ref, turner_ref, qb_ref, weight_ref, branch_ref):
    size = index_ref.shape[0]
    beta = 1.0 / (dist * size)
    entries = turner_ref.shape[1]
    for start in range(0, size, LANES):
        index = index_ref[:, start:start + LANES]
        found = jnp.zeros(index.shape, F32)
        for first in range(0, entries, LANES):
            table = jnp.exp(-turner_ref[:, first:first + LANES])
            table = jnp.broadcast_to(table, index.shape)
            inside = (index >= first) & (index < first + LANES)
            value = jnp.take_along_axis(table, jnp.where(inside, index - first, 0), axis=1)
            found = jnp.where(inside, value, found)
        weight_ref[:, start:start + LANES] = found
    total = jnp.zeros((size, size), F32)
    for level in range(1, dist):
        total = total + qb_ref[level - 1] * row(size, -(dist - level) * size, -beta)
    branch_ref[...] = jnp.sum(total, axis=1, keepdims=True)


def looked_up(table, me):
    entries = []
    for first in range(0, len(table), 7):
        lines = table[first:first + 7].astype(np.int64) + 1
        words = sum(line << (4 * at) for at, line in enumerate(lines))
        word = jnp.int32(0)
        for column, value in enumerate(words):
            word = jnp.where(me == column, jnp.int32(value), word)
        entries += [((word >> (4 * at)) & 15) - 1 for at in range(len(lines))]
    return entries


def pick_kernel(tables, *refs):
    me = lax.axis_index("row")
    sems = refs[-1]
    operands, places = refs[:len(tables)], refs[len(tables):-1]
    places = [ref.at[slot] for ref in places for slot in range(ref.shape[0])]
    copies = []
    for table, operand in zip(tables, operands):
        for entry in looked_up(table, me):
            number = len(copies)
            copy = pltpu.make_async_copy(operand.at[jnp.maximum(entry, 0)], places[number], sems.at[number])
            copies.append((entry >= 0, copy))
    for wanted, copy in copies:
        pl.when(wanted)(copy.start)
    for wanted, copy in copies:
        pl.when(wanted)(copy.wait)


def far_kernel(plan, dist, table_ref, qm1_ref, left_ref, *refs):
    me = lax.axis_index("row")
    rights, out_ref = refs[:-1], refs[-1]
    size = out_ref.shape[1]
    beta = 1.0 / (dist * size)
    out_ref[...] = jnp.zeros_like(out_ref)
    blocks = [rights[t].at[at] for t, at in plan.far_places]
    for number, right_ref in enumerate(blocks + [None]):
        slot = table_ref[plan.slots + number, me]

        @pl.when(slot >= 0)
        def _():
            m = table_ref[jnp.maximum(slot, 0), me]
            right = right_ref[...] if right_ref is not None else qm1_ref[dist - 1 - m]
            out_ref[:size] += product(left_ref[jnp.maximum(slot, 0)], right)
            out_ref[size:size + 1] += jnp.sum(right * column(size, m * size, beta), axis=0, keepdims=True)


def near_kernel(plan, dist, table_ref, qm_ref, *refs):
    me = lax.axis_index("row")
    rights, out_ref = refs[:-1], refs[-1]
    size = out_ref.shape[1]
    beta = 1.0 / (dist * size)
    out_ref[...] = jnp.zeros_like(out_ref)
    for number, (t, at) in enumerate(plan.places):
        right_ref = rights[t].at[at]
        m = table_ref[number, me]

        @pl.when(m >= 0)
        def _():
            right = right_ref[...]
            out_ref[:size] += product(qm_ref[m - 1], right)
            out_ref[size:size + 1] += jnp.sum(right * column(size, m * size, beta), axis=0, keepdims=True)


def last_kernel(plan, dist, near_ref, far_ref, weight_ref, branch_ref, own_ref, end_ref, pair_ref, qm1_ref, out_ref):
    live = lax.axis_index("row") < plan.lives
    size = weight_ref.shape[0]
    beta = 1.0 / (dist * size)

    @pl.when(jnp.logical_not(live))
    def _():
        for ref in (pair_ref, qm1_ref, out_ref):
            ref[...] = jnp.zeros_like(ref)

    @pl.when(live)
    def _():
        summed = near_ref[:size] + far_ref[:size]
        tail = near_ref[size:size + 1] + far_ref[size:size + 1]
        rows = lax.broadcasted_iota(jnp.int32, (size, size), 0)
        columns = lax.broadcasted_iota(jnp.int32, (size, size), 1)
        upper = jnp.where(rows <= columns, 1.0, 0.0).astype(BF16)
        own = jnp.sum(jnp.where(rows == columns, own_ref[...], 0), axis=1, keepdims=True)
        both = own + end_ref[...]
        allowed = (both == 3) | (both == 5)
        pair = jnp.where(allowed, weight_ref[...] * (1.0 + 0.8 * summed), 0.0)
        pair_ref[...] = pair
        high, low = halves(pair * row(size, 0, -beta))
        branch = (branch_ref[...] + (dot(high, upper) + dot(low, upper))) * (row(size, 0, beta) * beta)
        qm1_ref[...] = branch
        high, low = halves(branch * column(size, 0, beta))
        start = tail + (dot(upper, high) + dot(upper, low))
        out_ref[...] = summed + start * (0.01 * column(size, 0, -beta))


def per_device(qm, qm1, qb, codes, energy_index, turner):
    width = lax.axis_size("row")
    dist, size = qm.shape[2] + 1, qm.shape[3]
    plan = Plan(width, dist)
    qm, qm1, qb, index = qm[0, 0], qm1[0, 0], qb[0, 0], energy_index[0, 0]
    vmem = pl.BlockSpec(memory_space=pltpu.VMEM)
    smem = pl.BlockSpec(memory_space=pltpu.SMEM)
    hbm = pl.BlockSpec(memory_space=pltpu.HBM)
    square = jax.ShapeDtypeStruct((size, size), F32)
    tall = jax.ShapeDtypeStruct((size + 8, size), F32)

    def call(kernel, name, outs, ins, args, products, scratch=(), vmem_mib=40):
        many = isinstance(outs, tuple)
        return pl.pallas_call(
            kernel,
            out_shape=outs,
            in_specs=ins,
            out_specs=(vmem,) * len(outs) if many else vmem,
            scratch_shapes=scratch,
            compiler_params=pltpu.CompilerParams(vmem_limit_bytes=vmem_mib << 20),
            cost_estimate=pl.CostEstimate(
                flops=products * 6 * size**3, bytes_accessed=4 * size * size * (dist + 1), transcendentals=0
            ),
            name=name,
        )(*args)

    rounds = plan.rounds
    first = min(FIRST, rounds)
    stack = [jax.ShapeDtypeStruct((count, size, size), F32) for count in [plan.slots] + plan.sizes]
    cut = plan.starts[first]

    def pick(name, operands, tables, outs):
        lines = sum(len(table) for table in tables)
        return call(
            functools.partial(pick_kernel, tables), name, outs, [hbm] * len(operands), operands, 0,
            [pltpu.SemaphoreType.DMA((lines,))], 60,
        )

    picked = pick("pick_first", (qm, qm1), (plan.moved, plan.send[:cut]), tuple(stack[:first + 1]))
    left, blocks = picked[0], picked[1:]
    mid = min(LATE, rounds)
    end = plan.starts[mid]
    blocks += pick("pick_rest", (qm1,), (plan.send[cut:end],), tuple(stack[first + 1:mid + 1]))
    if rounds > mid:
        blocks += pick("pick_late", (qm1,), (plan.send[end:],), tuple(stack[mid + 1:]))
    left = lax.ppermute(left, "row", plan.there)
    early = [t for t in range(rounds) if t < LATE or t in plan.far_rounds]
    late = [t for t in range(rounds) if t not in early]
    rights = {t: lax.ppermute(blocks[t], "row", plan.pairs[t]) for t in early}
    own = codes[0]
    end = lax.ppermute(own, "row", [(i + dist, i) for i in range(plan.lives)])
    weight, branch = call(
        functools.partial(weights_kernel, dist), "weights", (square, jax.ShapeDtypeStruct((size, 1), F32)), [vmem] * 3,
        (index, jnp.pad(turner, (0, -turner.shape[0] % LANES))[None], qb), 0,
    )
    far = call(
        functools.partial(far_kernel, plan, dist), "far", tall, [smem] + [vmem] * (2 + len(plan.far_rounds)),
        (jnp.asarray(plan.far), qm1, left, *(rights[t] for t in plan.far_rounds)), 3,
    )
    if late:
        held, far = lax.optimization_barrier(([blocks[t] for t in late], far))
    else:
        held = [blocks[t] for t in late]
    far = lax.ppermute(far, "row", plan.back)
    rights.update((t, lax.ppermute(block, "row", plan.pairs[t])) for t, block in zip(late, held))
    near = call(
        functools.partial(near_kernel, plan, dist), "near", tall, [smem] + [vmem] * (1 + rounds),
        (jnp.asarray(plan.near), qm, *(rights[t] for t in range(rounds))), 20,
    )
    pair, branch, out = call(
        functools.partial(last_kernel, plan, dist), "last", (square,) * 3, [vmem] * 6,
        (near, far, weight, branch, own, end), 2,
    )
    return pair[None, None], branch[None, None], out[None, None]


def solution(mesh):
    blocks = P("seq", "row", None, None, None)
    return jax.shard_map(
        per_device,
        mesh=mesh,
        in_specs=(blocks, blocks, blocks, P("seq", "row", None), P("seq", "row", None, None), P()),
        out_specs=(P("seq", "row", None, None),) * 3,
        check_vma=False,
    )
```

```python
import functools

import jax
import jax.numpy as jnp
import numpy as np
from jax import lax
from jax.experimental import pallas as pl
from jax.experimental.pallas import tpu as pltpu
from jax.sharding import PartitionSpec as P

F32 = jnp.float32
BF16 = jnp.bfloat16
LANES = 128
FIRST = 1
LATE = 4
PLAN = (
    (5, (5, 6, 7), (1, 4, 2, 3, -1, 0, 1)),
    (3, (3, 4, 5), (1, 0, -1, 0, 1, 2, 3)),
    (5, (5, 6, 7), (1, 0, 2, 3, -1, 0, 1)),
    (3, (3, 4, 5), (2, 3, -1, 0, 1, 4, 1)),
    (4, (4, 5, 7), (0, 1, 3, -1, 2, 4, 0)),
    (4, (3, 4, 7), (0, 1, 2, -1, 3, 4, 0)),
    (5, (3, 6, 7), (0, 1, 0, 2, 3, 1, 2)),
    (3, (3, 4, 6), (0, 1, -1, 2, 4, 1, 2)),
)


def colored(flows):
    count = max(max(np.bincount([f[end] for f in flows])) for end in (0, 1))
    used = {}
    rounds = []
    for number, (source, target) in enumerate(flows):
        free = [[c for c in range(count) if (end, at, c) not in used] for end, at in ((0, source), (1, target))]
        common = [c for c in free[0] if c in free[1]]
        rounds.append(common[0] if common else free[0][0])
        if not common:
            first, second = free[0][0], free[1][0]
            chain, end, at, want = [], 1, target, first
            while (end, at, want) in used:
                other = used[end, at, want]
                chain.append(other)
                end, at = 1 - end, flows[other][1 - end]
                want = first + second - want
            for other in chain:
                for side in (0, 1):
                    del used[side, flows[other][side], rounds[other]]
            for other in chain:
                rounds[other] = first + second - rounds[other]
                for side in (0, 1):
                    used[side, flows[other][side], rounds[other]] = other
        for side in (0, 1):
            used[side, flows[number][side], rounds[number]] = number
    return rounds, count


class Plan:
    def __init__(self, width, dist):
        self.lives = lives = max(width - dist, 0)
        far = {}
        routes = {}
        for i in range(lives):
            offset, products, hints = PLAN[i % len(PLAN)]
            if i + offset < width and max(products) < dist:
                far[i] = (i + offset, products)
            for m in range(1, dist):
                at = far[i][0] if i in far and m in far[i][1] else i
                if at != i + m:
                    routes.setdefault((i + m, at), []).append((at == i, i, m, hints[m - 1] if m <= len(hints) else -1))
        rounds = {route: blocks[0][3] for route, blocks in routes.items()}
        ends = [(side, route[side], t) for route, t in rounds.items() for side in (0, 1)]
        if len(set(ends)) < len(ends) or min(rounds.values(), default=0) < 0:
            order = sorted(routes, key=lambda route: -len(routes[route]))
            rounds = dict(zip(order, colored(order)[0]))
        self.rounds = max(rounds.values(), default=-1) + 1
        self.pairs = [[route for route in routes if rounds[route] == t] for t in range(self.rounds)]
        self.sizes = [max(len(routes[route]) for route in pairs) for pairs in self.pairs]
        self.slots = slots = max([len(products) for _, products in far.values()], default=0)
        starts = np.concatenate([[0], np.cumsum(self.sizes)]).astype(int)
        self.send = np.full((starts[-1], width), -1, np.int32)
        self.near = np.full((starts[-1], width), -1, np.int32)
        far_slot = np.full((starts[-1], width), -1, np.int32)
        for (source, target), blocks in routes.items():
            for line, (is_near, i, m, _) in enumerate(sorted(blocks), starts[rounds[source, target]]):
                self.send[line, source] = dist - 1 - m
                if is_near:
                    self.near[line, target] = m
                else:
                    far_slot[line, target] = far[i][1].index(m)
        self.starts = starts
        self.places = [(t, at) for t, count in enumerate(self.sizes) for at in range(count)]
        lines = [line for line in range(starts[-1]) if far_slot[line].max() >= 0]
        self.far_rounds = sorted({self.places[line][0] for line in lines})
        self.far_places = [(self.far_rounds.index(t), at) for t, at in (self.places[line] for line in lines)]
        self.moved = np.full((slots, width), -1, np.int32)
        far_m = np.full((slots, width), -1, np.int32)
        own = np.full((1, width), -1, np.int32)
        for i, (at, products) in far.items():
            self.moved[:len(products), i] = np.array(products) - 1
            far_m[:len(products), at] = products
            if at - i in products:
                own[0, at] = products.index(at - i)
        self.far = np.concatenate([far_m, far_slot[lines], own])
        self.there = [(i, at) for i, (at, _) in far.items()]
        self.back = [(at, i) for i, at in self.there]


def halves(x):
    high = x.astype(BF16)
    return high, (x - high.astype(F32)).astype(BF16)


def dot(a, b):
    return jnp.dot(a, b, preferred_element_type=F32)


def product(left, right):
    left_high, left_low = halves(left)
    right_high, right_low = halves(right)
    return dot(left_high, right_high) + dot(left_high, right_low) + dot(left_low, right_high)


def column(size, start, beta):
    steps = lax.broadcasted_iota(jnp.int32, (size, 1), 0) + start
    return jnp.exp(steps.astype(F32) * -beta)


def row(size, start, beta):
    steps = lax.broadcasted_iota(jnp.int32, (1, size), 1) + start
    return jnp.exp(steps.astype(F32) * -beta)


def weights_kernel(dist, index_ref, turner_ref, qb_ref, weight_ref, branch_ref):
    size = index_ref.shape[0]
    beta = 1.0 / (dist * size)
    entries = turner_ref.shape[1]
    for start in range(0, size, LANES):
        index = index_ref[:, start:start + LANES]
        found = jnp.zeros(index.shape, F32)
        for first in range(0, entries, LANES):
            table = jnp.exp(-turner_ref[:, first:first + LANES])
            table = jnp.broadcast_to(table, index.shape)
            inside = (index >= first) & (index < first + LANES)
            value = jnp.take_along_axis(table, jnp.where(inside, index - first, 0), axis=1)
            found = jnp.where(inside, value, found)
        weight_ref[:, start:start + LANES] = found
    total = jnp.zeros((size, size), F32)
    for level in range(1, dist):
        total = total + qb_ref[level - 1] * row(size, -(dist - level) * size, -beta)
    branch_ref[...] = jnp.sum(total, axis=1, keepdims=True)


def looked_up(table, me):
    entries = []
    for first in range(0, len(table), 7):
        lines = table[first:first + 7].astype(np.int64) + 1
        words = sum(line << (4 * at) for at, line in enumerate(lines))
        word = jnp.int32(0)
        for column, value in enumerate(words):
            word = jnp.where(me == column, jnp.int32(value), word)
        entries += [((word >> (4 * at)) & 15) - 1 for at in range(len(lines))]
    return entries


def pick_kernel(tables, *refs):
    me = lax.axis_index("row")
    sems = refs[-1]
    operands, places = refs[:len(tables)], refs[len(tables):-1]
    places = [ref.at[slot] for ref in places for slot in range(ref.shape[0])]
    copies = []
    for table, operand in zip(tables, operands):
        for entry in looked_up(table, me):
            number = len(copies)
            copy = pltpu.make_async_copy(operand.at[jnp.maximum(entry, 0)], places[number], sems.at[number])
            copies.append((entry >= 0, copy))
    for wanted, copy in copies:
        pl.when(wanted)(copy.start)
    for wanted, copy in copies:
        pl.when(wanted)(copy.wait)


def far_kernel(plan, dist, table_ref, qm1_ref, left_ref, *refs):
    me = lax.axis_index("row")
    rights, out_ref = refs[:-1], refs[-1]
    size = out_ref.shape[1]
    beta = 1.0 / (dist * size)
    out_ref[...] = jnp.zeros_like(out_ref)
    blocks = [rights[t].at[at] for t, at in plan.far_places]
    for number, right_ref in enumerate(blocks + [None]):
        slot = table_ref[plan.slots + number, me]

        @pl.when(slot >= 0)
        def _():
            m = table_ref[jnp.maximum(slot, 0), me]
            right = right_ref[...] if right_ref is not None else qm1_ref[dist - 1 - m]
            out_ref[:size] += product(left_ref[jnp.maximum(slot, 0)], right)
            out_ref[size:size + 1] += jnp.sum(right * column(size, m * size, beta), axis=0, keepdims=True)


def near_kernel(plan, dist, table_ref, qm_ref, *refs):
    me = lax.axis_index("row")
    rights, out_ref = refs[:-1], refs[-1]
    size = out_ref.shape[1]
    beta = 1.0 / (dist * size)
    out_ref[...] = jnp.zeros_like(out_ref)
    for number, (t, at) in enumerate(plan.places):
        right_ref = rights[t].at[at]
        m = table_ref[number, me]

        @pl.when(m >= 0)
        def _():
            right = right_ref[...]
            out_ref[:size] += product(qm_ref[m - 1], right)
            out_ref[size:size + 1] += jnp.sum(right * column(size, m * size, beta), axis=0, keepdims=True)


def last_kernel(plan, dist, near_ref, far_ref, weight_ref, branch_ref, own_ref, end_ref, pair_ref, qm1_ref, out_ref):
    live = lax.axis_index("row") < plan.lives
    size = weight_ref.shape[0]
    beta = 1.0 / (dist * size)

    @pl.when(jnp.logical_not(live))
    def _():
        for ref in (pair_ref, qm1_ref, out_ref):
            ref[...] = jnp.zeros_like(ref)

    @pl.when(live)
    def _():
        summed = near_ref[:size] + far_ref[:size]
        tail = near_ref[size:size + 1] + far_ref[size:size + 1]
        rows = lax.broadcasted_iota(jnp.int32, (size, size), 0)
        columns = lax.broadcasted_iota(jnp.int32, (size, size), 1)
        upper = jnp.where(rows <= columns, 1.0, 0.0).astype(BF16)
        own = jnp.sum(jnp.where(rows == columns, own_ref[...], 0), axis=1, keepdims=True)
        both = own + end_ref[...]
        allowed = (both == 3) | (both == 5)
        pair = jnp.where(allowed, weight_ref[...] * (1.0 + 0.8 * summed), 0.0)
        pair_ref[...] = pair
        high, low = halves(pair * row(size, 0, -beta))
        branch = (branch_ref[...] + (dot(high, upper) + dot(low, upper))) * (row(size, 0, beta) * beta)
        qm1_ref[...] = branch
        high, low = halves(branch * column(size, 0, beta))
        start = tail + (dot(upper, high) + dot(upper, low))
        out_ref[...] = summed + start * (0.01 * column(size, 0, -beta))


def per_device(qm, qm1, qb, codes, energy_index, turner):
    width = lax.axis_size("row")
    dist, size = qm.shape[2] + 1, qm.shape[3]
    plan = Plan(width, dist)
    qm, qm1, qb, index = qm[0, 0], qm1[0, 0], qb[0, 0], energy_index[0, 0]
    vmem = pl.BlockSpec(memory_space=pltpu.VMEM)
    smem = pl.BlockSpec(memory_space=pltpu.SMEM)
    hbm = pl.BlockSpec(memory_space=pltpu.HBM)
    square = jax.ShapeDtypeStruct((size, size), F32)
    tall = jax.ShapeDtypeStruct((size + 8, size), F32)

    def call(kernel, name, outs, ins, args, products, scratch=(), vmem_mib=40):
        many = isinstance(outs, tuple)
        return pl.pallas_call(
            kernel,
            out_shape=outs,
            in_specs=ins,
            out_specs=(vmem,) * len(outs) if many else vmem,
            scratch_shapes=scratch,
            compiler_params=pltpu.CompilerParams(vmem_limit_bytes=vmem_mib << 20),
            cost_estimate=pl.CostEstimate(
                flops=products * 6 * size**3, bytes_accessed=4 * size * size * (dist + 1), transcendentals=0
            ),
            name=name,
        )(*args)

    rounds = plan.rounds
    first = min(FIRST, rounds)
    stack = [jax.ShapeDtypeStruct((count, size, size), F32) for count in [plan.slots] + plan.sizes]
    cut = plan.starts[first]

    def pick(name, operands, tables, outs):
        lines = sum(len(table) for table in tables)
        return call(
            functools.partial(pick_kernel, tables), name, outs, [hbm] * len(operands), operands, 0,
            [pltpu.SemaphoreType.DMA((lines,))], 60,
        )

    picked = pick("pick_first", (qm, qm1), (plan.moved, plan.send[:cut]), tuple(stack[:first + 1]))
    left, blocks = picked[0], picked[1:]
    mid = min(LATE, rounds)
    end = plan.starts[mid]
    blocks += pick("pick_rest", (qm1,), (plan.send[cut:end],), tuple(stack[first + 1:mid + 1]))
    if rounds > mid:
        blocks += pick("pick_late", (qm1,), (plan.send[end:],), tuple(stack[mid + 1:]))
    left = lax.ppermute(left, "row", plan.there)
    early = [t for t in range(rounds) if t < LATE or t in plan.far_rounds]
    late = [t for t in range(rounds) if t not in early]
    rights = {t: lax.ppermute(blocks[t], "row", plan.pairs[t]) for t in early}
    own = codes[0]
    end = lax.ppermute(own, "row", [(i + dist, i) for i in range(plan.lives)])
    weight, branch = call(
        functools.partial(weights_kernel, dist), "weights", (square, jax.ShapeDtypeStruct((size, 1), F32)), [vmem] * 3,
        (index, jnp.pad(turner, (0, -turner.shape[0] % LANES))[None], qb), 0,
    )
    far = call(
        functools.partial(far_kernel, plan, dist), "far", tall, [smem] + [vmem] * (2 + len(plan.far_rounds)),
        (jnp.asarray(plan.far), qm1, left, *(rights[t] for t in plan.far_rounds)), 3,
    )
    if late:
        held, far = lax.optimization_barrier(([blocks[t] for t in late], far))
    else:
        held = [blocks[t] for t in late]
    far = lax.ppermute(far, "row", plan.back)
    rights.update((t, lax.ppermute(block, "row", plan.pairs[t])) for t, block in zip(late, held))
    near = call(
        functools.partial(near_kernel, plan, dist), "near", tall, [smem] + [vmem] * (1 + rounds),
        (jnp.asarray(plan.near), qm, *(rights[t] for t in range(rounds))), 20,
    )
    pair, branch, out = call(
        functools.partial(last_kernel, plan, dist), "last", (square,) * 3, [vmem] * 6,
        (near, far, weight, branch, own, end), 2,
    )
    return pair[None, None], branch[None, None], out[None, None]


def solution(mesh):
    blocks = P("seq", "row", None, None, None)
    return jax.shard_map(
        per_device,
        mesh=mesh,
        in_specs=(blocks, blocks, blocks, P("seq", "row", None), P("seq", "row", None, None), P()),
        out_specs=(P("seq", "row", None, None),) * 3,
        check_vma=False,
    )
```
